256 devices in a mesh: tm: 16 (over y_hi, x, core), rows: 16 (over z, y_lo).
Axes of the slice: x: 4, y: 4 (y_hi: 2, y_lo: 2; y = y_hi * 2 + y_lo), z: 8, core: 2. Of those that a mesh axis runs over, the one named last changes fastest.
Arguments:
- frames: bfloat16 [64, 256, 3072], P('tm', 'rows'), may hold values from -6 to 6
- gain_one: float32 [96], replicated, may hold values from 0.5 to 1.5
- weight_one: bfloat16 [3, 3, 3, 96, 96], replicated, may hold values from -0.125 to 0.125
- bias_one: float32 [96], replicated, may hold values from -1.5 to 1.5
- gain_two: float32 [96], replicated, may hold values from 0.5 to 1.5
- weight_two: bfloat16 [3, 3, 3, 96, 96], replicated, may hold values from -0.125 to 0.125
- bias_two: float32 [96], replicated, may hold values from -1.5 to 1.5
Outputs:
- block_out: bfloat16 [64, 256, 3072], P('tm', 'rows')
The draws below stay inside these ranges and needn't reach their ends.
All inputs are finite; a program needn't handle non-finite values.
Results may differ from the reference program's by a relative error of at most 0.0047.
Values may be sent and summed in bfloat16 or wider, within the bound.
No kernel may reach another device: no remote copies, remote signals or barrier semaphores. Data moves between devices by JAX's collectives and lax.ppermute only.
A program may use at most 64 MiB of HBM per device.

```python
import jax
import jax.numpy as jnp
from jax import lax

C = 96
GROUP = 4
COLS = 32
FRAMES = 64
HEIGHT = 256


def shard_levels(own_key, dims, shards, low, top_value):
    def one(dim, shards_of):
        steps = jax.random.uniform(jax.random.fold_in(jax.random.fold_in(own_key, 6), dim), (shards_of,), jnp.float32, low / len(shards), top_value / len(shards))
        return jnp.repeat(jnp.exp(steps), dims[dim] // shards_of).reshape((-1,) + (1,) * (len(dims) - dim - 1))

    factor_of = one(*shards[0])
    for cut in shards[1:]:
        factor_of = factor_of * one(*cut)
    return factor_of


def gaussian(key, dims, scale, limit, pieces=(), held_as=jnp.bfloat16):
    factor_of = shard_levels(key, dims, pieces, -0.22, 0.18) if pieces else 1.0
    array = jax.random.normal(key, dims, jnp.float32) * scale * factor_of
    return jnp.minimum(jnp.maximum(array, -limit), limit).astype(held_as)


def setup_inputs(seed: int = 0) -> dict:
    streams_of = jax.random.split(jax.random.key(seed), 8)
    return {
        "frames": gaussian(streams_of[0], (FRAMES, HEIGHT, COLS * C), 1.0, 6.0, ((0, 16), (1, 16))),
        "gain_one": jnp.clip(jax.random.uniform(streams_of[1], (C,), jnp.float32, 0.5, 1.5), 0.5, 1.5),
        "weight_one": gaussian(streams_of[2], (3, 3, 3, C, C), (27 * C) ** -0.5, 0.125),
        "bias_one": gaussian(streams_of[3], (C,), 0.3, 1.5, (), jnp.float32),
        "gain_two": jnp.clip(jax.random.uniform(streams_of[4], (C,), jnp.float32, 0.5, 1.5), 0.5, 1.5),
        "weight_two": gaussian(streams_of[5], (3, 3, 3, C, C), (27 * C) ** -0.5, 0.125),
        "bias_two": gaussian(streams_of[6], (C,), 0.3, 1.5, (), jnp.float32),
    }


def norm_act(value, gain):
    mean_sq = lax.optimization_barrier(jnp.mean(value * value, axis=-1, keepdims=True))
    return jax.nn.silu(value * lax.rsqrt(mean_sq + 1e-06) * gain)

def causal_conv(act, weight):
    padded = jnp.pad(act, ((2, 0), (1, 1), (1, 1), (0, 0)))
    kernel = weight.astype(jnp.float32)
    starts = jnp.arange(FRAMES // GROUP, dtype=jnp.int32) * GROUP

    def one_block(start):
        zero = jnp.zeros((), jnp.int32)
        piece = lax.dynamic_slice(padded, (start, zero, zero, zero), (GROUP + 2, HEIGHT + 2, COLS + 2, C))
        result = lax.conv_general_dilated(piece[None].astype(jnp.float32), kernel, (1, 1, 1), 'VALID', dimension_numbers=('NDHWC', 'DHWIO', 'NDHWC'), precision=lax.Precision.HIGHEST)
        return result[0]
    blocks = lax.map(one_block, starts)
    return blocks.reshape(FRAMES, HEIGHT, COLS, C)

def reference(frames, gain_one, weight_one, bias_one, gain_two, weight_two, bias_two):
    inputs = frames.reshape(FRAMES, HEIGHT, COLS, C).astype(jnp.float32)
    act_one = norm_act(inputs, gain_one).astype(jnp.bfloat16)
    hidden = (causal_conv(act_one, weight_one) + bias_one).astype(jnp.bfloat16)
    hidden = lax.optimization_barrier(hidden)
    act_two = norm_act(hidden.astype(jnp.float32), gain_two).astype(jnp.bfloat16)
    result = inputs + causal_conv(act_two, weight_two) + bias_two
    return result.astype(jnp.bfloat16).reshape(FRAMES, HEIGHT, COLS * C)
```

```python
import jax
import jax.numpy as jnp
from jax import lax
from jax.experimental import pallas as pl
from jax.experimental.pallas import tpu as pltpu
from jax.sharding import PartitionSpec as P

C = 96
GROUP = 768
PAD = 128
LANES = 3072
WIDE = LANES + 2 * PAD
STARTS = (-128, 0, 384)
DEPTHS = (512, 768, 512)
HALVES = (
    ((96, (32, 0), (128, 96)), (64, (128, 96), (224, 64))),
    ((32, (96, 64), (192, 32)), (96, (288, 0), (384, 96))),
    ((64, (0, 96), (96, 64)), (32, (96, 64), (192, 32))),
)
BF = jnp.bfloat16
F32 = jnp.float32


def edges_kernel(x_ref, e0_ref, e1_ref):
    even = lax.rem(lax.axis_index("rows"), 2) == 0
    top, bot = [], []
    for row in range(2):
        for f in range(4):
            top.append(x_ref[f, 0:8, :].astype(F32)[row : row + 1])
    for row in range(2):
        for f in range(4):
            bot.append(x_ref[f, 8:16, :].astype(F32)[6 + row : 7 + row])
    top = jnp.concatenate(top, axis=0)
    bot = jnp.concatenate(bot, axis=0)
    e0_ref[...] = jnp.where(even, bot, top).astype(BF)
    e1_ref[...] = jnp.where(even, top, bot).astype(BF)


def band_kernel(w_ref, o0_ref, o1_ref, o2_ref):
    src = lax.broadcasted_iota(jnp.int32, (C, 256), 0)
    dst = lax.broadcasted_iota(jnp.int32, (C, 256), 1)

    def place(low, high):
        lane = lax.rem(dst, 128)
        turn = jnp.where(dst < 128, low, high)
        return jnp.where(lax.rem(src + turn, 128) == lane, 1.0, 0.0).astype(BF)

    first, second = place(0, 32), place(64, 96)
    outs = (o0_ref, o1_ref, o2_ref)

    def tap(k, carry):
        block = w_ref[pl.ds(3 * k, 3)].reshape(3 * C, C)
        a = jnp.dot(block, first, preferred_element_type=F32).astype(BF)
        b = jnp.dot(block, second, preferred_element_type=F32).astype(BF)
        turned = {0: a[:, :128], 32: a[:, 128:], 64: b[:, :128], 96: b[:, 128:]}
        for p in range(3):
            for half in range(2):
                edge, left, right = HALVES[p][half]

                def at(spot):
                    row, turn = spot
                    parts = [turned[turn]]
                    if row:
                        parts.insert(0, jnp.zeros((row, 128), BF))
                    rest = DEPTHS[p] - row - 3 * C
                    if rest:
                        parts.append(jnp.zeros((rest, 128), BF))
                    return jnp.concatenate(parts, axis=0)

                lane = lax.broadcasted_iota(jnp.int32, (DEPTHS[p], 128), 1)
                outs[p][k, :, 128 * half : 128 * half + 128] = jnp.where(lane < edge, at(left), at(right))
        return carry

    lax.fori_loop(0, 9, tap, 0)


def main_kernel(
    x_ref, prev_ref, h0_ref, h1_ref, c_ref, par_ref,
    u0, u1, u2, v0, v1, v2, out_ref,
    s1, a1, e, et, hid, hide, s2, a2,
):
    tm = lax.axis_index("tm")
    rows = lax.axis_index("rows")
    even = lax.rem(rows, 2) == 0
    lane = lax.broadcasted_iota(jnp.int32, (GROUP, 128), 0)
    col = lax.broadcasted_iota(jnp.int32, (GROUP, 128), 1)
    gather = jnp.where((lane >= col * C) & (lane < col * C + C), 1.0, 0.0).astype(BF)
    lane = lax.broadcasted_iota(jnp.int32, (256, GROUP), 1)
    col = lax.rem(lax.broadcasted_iota(jnp.int32, (256, GROUP), 0), 128)
    spread = jnp.where((lane >= col * C) & (lane < col * C + C), 1.0, 0.0).astype(BF)

    def act(v, gain):
        total = jnp.dot((v * v).astype(BF), gather, preferred_element_type=F32)
        r = lax.rsqrt(total * (1.0 / C) + 1e-06)
        high = r.astype(BF)
        low = (r - high.astype(F32)).astype(BF)
        wide = jnp.dot(jnp.concatenate([high, low], axis=1), spread, preferred_element_type=F32)
        half = v * wide * gain
        return half + half * jnp.tanh(half)

    def zero_sides(ref, index):
        shape = ref.shape[len(index) : -1]
        ref[index + (Ellipsis, pl.ds(0, PAD))] = jnp.zeros(shape + (PAD,), BF)
        ref[index + (Ellipsis, pl.ds(PAD + LANES, PAD))] = jnp.zeros(shape + (PAD,), BF)

    zero_sides(a1, ())
    zero_sides(et, ())
    zero_sides(a2, ())

    gain1 = par_ref[0:1, :]
    bias1 = par_ref[1:2, :]
    gain2 = par_ref[2:3, :]
    bias2 = par_ref[3:4, :]
    older = tm > 0

    for g in range(4):
        cut = pl.ds(GROUP * g, GROUP)
        h0, h1 = h0_ref[:, cut].astype(F32), h1_ref[:, cut].astype(F32)
        c0, c1 = c_ref[0:8, cut].astype(F32), c_ref[8:16, cut].astype(F32)
        up = jnp.where(rows > 0, jnp.where(even, h1, h0), 0.0)
        down = jnp.where(rows < 15, jnp.where(even, h0, h1), 0.0)
        up_old = jnp.where((rows > 0) & older, jnp.where(even, c1, c0), 0.0)
        down_old = jnp.where((rows < 15) & older, jnp.where(even, c0, c1), 0.0)
        both = act(jnp.concatenate([up_old, up, down_old, down], axis=0), gain1)
        e[0, 0:8, cut] = jnp.concatenate([both[0:4], both[8:12]], axis=0)
        e[1, 0:8, cut] = jnp.concatenate([both[4:8], both[12:16]], axis=0)
        e[4, 0:8, cut] = jnp.concatenate([both[16:20], both[24:28]], axis=0)
        e[5, 0:8, cut] = jnp.concatenate([both[20:24], both[28:32]], axis=0)

    for f in range(8):
        for g in range(4):
            cut = pl.ds(GROUP * g, GROUP)
            if f < 4:
                v = jnp.where(older, prev_ref[f, :, cut].astype(F32), 0.0)
            else:
                v = x_ref[f - 4, :, cut].astype(F32)
            s1[f, 8:24, cut] = act(v, gain1)
    for f in range(8):
        s1[f, 7:8, :] = e[1, f : f + 1, :]
        s1[f, 24:25, :] = e[4, f : f + 1, :]
        e[2, f : f + 1, :] = s1[f, 8:9, :]
        e[3, f : f + 1, :] = s1[f, 23:24, :]
    inner = pl.ds(PAD, LANES)
    for f in range(8):
        for kh in range(3):
            a1[kh, f, :, inner] = s1[f, 7 + kh : 23 + kh, :].astype(BF)
    for kt in range(3):
        for kh in range(3):
            et[kt, kh, :, inner] = jnp.concatenate(
                [e[kh, kt : kt + 8, :], e[3 + kh, kt : kt + 8, :]], axis=0
            ).astype(BF)

    for p, w in enumerate((u0, u1, u2)):
        depth = DEPTHS[p]
        taps = []
        for kt in range(3):
            for kh in range(3):
                parts = []
                for g in range(4):
                    cut = pl.ds(PAD + GROUP * g + STARTS[p], depth)
                    parts.append(a1[kh, kt : kt + 6, :, cut].reshape(96, depth))
                for g in range(4):
                    cut = pl.ds(PAD + GROUP * g + STARTS[p], depth)
                    parts.append(et[kt, kh, :, cut])
                taps.append(jnp.concatenate(parts, axis=0))
        total = jnp.dot(
            jnp.concatenate(taps, axis=1), w[...].reshape(9 * depth, 256), preferred_element_type=F32
        )
        total = (total + bias1[:, 256 * p : 256 * p + 256]).astype(BF)
        for g in range(4):
            cut = pl.ds(GROUP * g + 256 * p, 256)
            hid[:, :, cut] = total[96 * g : 96 * g + 96].reshape(6, 16, 256)
            hide[:, cut] = total[384 + 16 * g : 400 + 16 * g]

    spot = lax.broadcasted_iota(jnp.int32, (16, GROUP), 0)
    frame = lax.rem(spot, 8)
    keep = ((spot >= 8) | (rows > 0)) & ((spot < 8) | (rows < 15)) & ((frame >= 2) | older)
    for f in range(6):
        for g in range(4):
            cut = pl.ds(GROUP * g, GROUP)
            v = act(hid[f, :, cut].astype(F32), gain2)
            if f < 2:
                v = jnp.where(older, v, 0.0)
            s2[f, 8:24, cut] = v
    for g in range(4):
        cut = pl.ds(GROUP * g, GROUP)
        e[0, :, cut] = jnp.where(keep, act(hide[:, cut].astype(F32), gain2), 0.0)
    for f in range(6):
        s2[f, 7:8, :] = e[0, f : f + 1, :]
        s2[f, 24:25, :] = e[0, 8 + f : 9 + f, :]
    for f in range(6):
        for kh in range(3):
            a2[kh, f, :, inner] = s2[f, 7 + kh : 23 + kh, :].astype(BF)

    for p, w in enumerate((v0, v1, v2)):
        depth = DEPTHS[p]
        taps = []
        for kt in range(3):
            for kh in range(3):
                parts = []
                for g in range(4):
                    cut = pl.ds(PAD + GROUP * g + STARTS[p], depth)
                    parts.append(a2[kh, kt : kt + 4, :, cut].reshape(64, depth))
                taps.append(jnp.concatenate(parts, axis=0))
        total = jnp.dot(
            jnp.concatenate(taps, axis=1), w[...].reshape(9 * depth, 256), preferred_element_type=F32
        )
        total = total + bias2[:, 256 * p : 256 * p + 256]
        for g in range(4):
            cut = pl.ds(GROUP * g + 256 * p, 256)
            out_ref[:, :, cut] = (
                x_ref[:, :, cut].astype(F32) + total[64 * g : 64 * g + 64].reshape(4, 16, 256)
            ).astype(BF)


def vmem():
    return pl.BlockSpec(memory_space=pltpu.VMEM)


def make_pairs(tms, rws):
    def flat(move):
        pairs = []
        for t in range(tms):
            for r in range(rws):
                to_t, to_r = move(t, r)
                pairs.append((t * rws + r, to_t * rws + to_r))
        return pairs

    def odd(t, r):
        if r in (0, rws - 1):
            return t ^ 1, r
        return t, (r + 1 if r % 2 else r - 1)

    return (
        flat(lambda t, r: (t, r ^ 1)),
        flat(odd),
        flat(lambda t, r: ((t + 1) % tms, r)),
    )


def solution(mesh):
    even_swap, odd_swap, later = make_pairs(mesh.shape["tm"], mesh.shape["rows"])
    axes = ("tm", "rows")

    def body(frames, gain_one, weight_one, bias_one, gain_two, weight_two, bias_two):
        prev = lax.ppermute(frames, axes, later)
        edge = jax.ShapeDtypeStruct((8, LANES), BF)
        e0, e1 = pl.pallas_call(
            edges_kernel, out_shape=(edge, edge), in_specs=[vmem()], out_specs=(vmem(), vmem()), name="edges"
        )(frames)
        h0 = lax.ppermute(e0, axes, even_swap)
        h1 = lax.ppermute(e1, axes, odd_swap)
        corners = lax.ppermute(jnp.concatenate([h0, h1], axis=0), axes, later)
        params = jnp.stack([0.5 * gain_one, bias_one, 0.5 * gain_two, bias_two])
        params = jnp.tile(params, (1, GROUP // C))

        def bands(w):
            return pl.pallas_call(
                band_kernel,
                out_shape=tuple(pltpu.VMEM((9, d, 256), BF) for d in DEPTHS),
                in_specs=[vmem()],
                out_specs=(vmem(),) * 3,
                compiler_params=pltpu.CompilerParams(vmem_limit_bytes=8 << 20),
                name="bands",
            )(w.reshape(27, C, C))

        u = bands(weight_one)
        v = bands(weight_two)
        return pl.pallas_call(
            main_kernel,
            out_shape=jax.ShapeDtypeStruct((4, 16, LANES), BF),
            in_specs=[vmem()] * 12,
            out_specs=vmem(),
            scratch_shapes=[
                pltpu.VMEM((8, 32, LANES), F32),
                pltpu.VMEM((3, 8, 16, WIDE), BF),
                pltpu.VMEM((6, 16, LANES), F32),
                pltpu.VMEM((3, 3, 16, WIDE), BF),
                pltpu.VMEM((6, 16, LANES), BF),
                pltpu.VMEM((16, LANES), BF),
                pltpu.VMEM((6, 32, LANES), F32),
                pltpu.VMEM((3, 6, 16, WIDE), BF),
            ],
            compiler_params=pltpu.CompilerParams(vmem_limit_bytes=40 << 20),
            name="block",
        )(frames, prev, h0, h1, corners, params, *u, *v)

    in_specs = (P("tm", "rows", None), P(), P(), P(), P(), P(), P())
    out_specs = P("tm", "rows", None)
    return jax.shard_map(body, mesh=mesh, in_specs=in_specs, out_specs=out_specs, check_vma=False)
```

```python
import jax
import jax.numpy as jnp
from jax import lax
from jax.experimental import pallas as pl
from jax.experimental.pallas import tpu as pltpu
from jax.sharding import PartitionSpec as P

C = 96
GROUP = 768
PAD = 128
LANES = 3072
WIDE = LANES + 2 * PAD
STARTS = (-128, 0, 384)
DEPTHS = (512, 768, 512)
HALVES = (
    ((96, (32, 0), (128, 96)), (64, (128, 96), (224, 64))),
    ((32, (96, 64), (192, 32)), (96, (288, 0), (384, 96))),
    ((64, (0, 96), (96, 64)), (32, (96, 64), (192, 32))),
)
BF = jnp.bfloat16
F32 = jnp.float32


def edges_kernel(x_ref, e0_ref, e1_ref):
    even = lax.rem(lax.axis_index("rows"), 2) == 0
    top, bot = [], []
    for row in range(2):
        for f in range(4):
            top.append(x_ref[f, 0:8, :].astype(F32)[row : row + 1])
    for row in range(2):
        for f in range(4):
            bot.append(x_ref[f, 8:16, :].astype(F32)[6 + row : 7 + row])
    top = jnp.concatenate(top, axis=0)
    bot = jnp.concatenate(bot, axis=0)
    e0_ref[...] = jnp.where(even, bot, top).astype(BF)
    e1_ref[...] = jnp.where(even, top, bot).astype(BF)


def band_kernel(
    w1_ref, w2_ref, p0, p1, p2, p3, o0, o1, o2, q0, q1, q2, par_ref, buf, small, sems, small_sems
):
    tiny = []
    for n, ref in enumerate((p0, p1, p2, p3)):
        tiny.append(pltpu.make_async_copy(ref, small.at[n], small_sems.at[n]))
        tiny[-1].start()
    copies = []
    for n, ref in enumerate((w1_ref, w2_ref)):
        for k in range(3):
            copies.append(pltpu.make_async_copy(ref.at[k], buf.at[n, k], sems.at[n, k]))
            copies[-1].start()
    src = lax.broadcasted_iota(jnp.int32, (C, 256), 0)
    dst = lax.broadcasted_iota(jnp.int32, (C, 256), 1)

    def place(low, high):
        lane = lax.rem(dst, 128)
        turn = jnp.where(dst < 128, low, high)
        return jnp.where(lax.rem(src + turn, 128) == lane, 1.0, 0.0).astype(BF)

    first, second = place(0, 32), place(64, 96)
    for n, outs in enumerate(((o0, o1, o2), (q0, q1, q2))):
        for kt in range(3):
            copies[3 * n + kt].wait()
            block = buf[n, kt].reshape(9 * C, C)
            a = jnp.dot(block, first, preferred_element_type=F32).astype(BF)
            b = jnp.dot(block, second, preferred_element_type=F32).astype(BF)
            for kh in range(3):
                part = slice(3 * C * kh, 3 * C * kh + 3 * C)
                turned = {0: a[part, :128], 32: a[part, 128:], 64: b[part, :128], 96: b[part, 128:]}
                for p in range(3):
                    for half in range(2):
                        edge, left, right = HALVES[p][half]

                        def at(spot):
                            row, turn = spot
                            parts = [turned[turn]]
                            if row:
                                parts.insert(0, jnp.zeros((row, 128), BF))
                            rest = DEPTHS[p] - row - 3 * C
                            if rest:
                                parts.append(jnp.zeros((rest, 128), BF))
                            return jnp.concatenate(parts, axis=0)

                        lane = lax.broadcasted_iota(jnp.int32, (DEPTHS[p], 128), 1)
                        outs[p][3 * kt + kh, :, 128 * half : 128 * half + 128] = jnp.where(
                            lane < edge, at(left), at(right)
                        )
    for copy in tiny:
        copy.wait()
    params = jnp.concatenate([0.5 * small[0], small[1], 0.5 * small[2], small[3]], axis=0)
    par_ref[...] = jnp.concatenate([params] * (GROUP // C), axis=1)


def bands(weight_one, weight_two, params):
    far = [weight_one.reshape(3, 9, C, C), weight_two.reshape(3, 9, C, C)] + [q.reshape(1, C) for q in params]
    far = [pltpu.with_memory_space_constraint(q, pltpu.HBM) for q in far]
    return pl.pallas_call(
        band_kernel,
        out_shape=tuple(pltpu.VMEM((9, d, 256), BF) for d in DEPTHS * 2) + (pltpu.VMEM((4, GROUP), F32),),
        in_specs=[pl.BlockSpec(memory_space=pltpu.HBM)] * 6,
        out_specs=(vmem(),) * 7,
        scratch_shapes=[
            pltpu.VMEM((2, 3, 9, C, C), BF),
            pltpu.VMEM((4, 1, C), F32),
            pltpu.SemaphoreType.DMA((2, 3)),
            pltpu.SemaphoreType.DMA((4,)),
        ],
        compiler_params=pltpu.CompilerParams(vmem_limit_bytes=8 << 20),
        cost_estimate=pl.CostEstimate(flops=4000000000, bytes_accessed=18000000, transcendentals=0),
        name="bands",
    )(*far)


def main_kernel(
    x_ref, prev_ref, h0_ref, h1_ref, c0_ref, c1_ref,
    u0, u1, u2, v0, v1, v2, par_ref, out_ref,
    square, scale, a1, e, et, hid, a2,
):
    tm = lax.axis_index("tm")
    rows = lax.axis_index("rows")
    even = lax.rem(rows, 2) == 0
    older = tm > 0
    lane = lax.broadcasted_iota(jnp.int32, (GROUP, 128), 0)
    col = lax.broadcasted_iota(jnp.int32, (GROUP, 128), 1)
    gather = jnp.where((lane >= col * C) & (lane < col * C + C), 1.0, 0.0).astype(BF)
    lane = lax.broadcasted_iota(jnp.int32, (256, GROUP), 1)
    col = lax.rem(lax.broadcasted_iota(jnp.int32, (256, GROUP), 0), 128)
    spread = jnp.where((lane >= col * C) & (lane < col * C + C), 1.0, 0.0).astype(BF)

    def norm(count):
        total = jnp.dot(square[0:count, :], gather, preferred_element_type=F32)
        r = lax.rsqrt(total * (1.0 / C) + 1e-06)
        high = r.astype(BF)
        low = (r - high.astype(F32)).astype(BF)
        scale[0:count, :] = jnp.dot(jnp.concatenate([high, low], axis=1), spread, preferred_element_type=F32)

    def act(v, where, gain):
        half = v.astype(F32) * scale[where, :] * gain
        return half + half * jnp.tanh(half)

    def zero_sides(ref):
        shape = ref.shape[:-1]
        ref[..., pl.ds(0, PAD)] = jnp.zeros(shape + (PAD,), BF)
        ref[..., pl.ds(PAD + LANES, PAD)] = jnp.zeros(shape + (PAD,), BF)

    zero_sides(a1)
    zero_sides(et)
    zero_sides(a2)

    gain1 = par_ref[0:1, :]
    bias1 = par_ref[1:2, :]
    gain2 = par_ref[2:3, :]
    bias2 = par_ref[3:4, :]

    def shifted(ref, f, g, v, above, below):
        cut = pl.ds(PAD + GROUP * g, GROUP)
        ref[0, f, :, cut] = jnp.concatenate([above, v[0:15]], axis=0).astype(BF)
        ref[1, f, :, cut] = v.astype(BF)
        ref[2, f, :, cut] = jnp.concatenate([v[1:16], below], axis=0).astype(BF)

    zero = jnp.zeros((), BF)
    halos = []
    for g in range(4):
        cut = pl.ds(GROUP * g, GROUP)
        h0, h1 = h0_ref[:, cut].astype(F32), h1_ref[:, cut].astype(F32)
        c0, c1 = c0_ref[:, cut].astype(F32), c1_ref[:, cut].astype(F32)
        up = jnp.where(rows > 0, jnp.where(even, h1, h0), 0.0)
        down = jnp.where(rows < 15, jnp.where(even, h0, h1), 0.0)
        up_old = jnp.where((rows > 0) & older, jnp.where(even, c1, c0), 0.0)
        down_old = jnp.where((rows < 15) & older, jnp.where(even, c0, c1), 0.0)
        halo = jnp.concatenate([up_old, up, down_old, down], axis=0).astype(BF)
        e[0, 0:8, cut] = up_old
        e[1, 0:8, cut] = up
        e[4, 0:8, cut] = down_old
        e[5, 0:8, cut] = down
        before = jnp.where(older, prev_ref[:, :, cut].reshape(64, GROUP), zero)
        own = x_ref[:, :, cut].reshape(64, GROUP)
        square[160 * g : 160 * g + 64, :] = before * before
        square[160 * g + 64 : 160 * g + 128, :] = own * own
        square[160 * g + 128 : 160 * g + 160, :] = halo * halo
    norm(640)
    for g in range(4):
        cut = pl.ds(GROUP * g, GROUP)
        at = 160 * g + 128
        up_old = act(e[0, 0:8, cut], pl.ds(at, 8), gain1)
        up = act(e[1, 0:8, cut], pl.ds(at + 8, 8), gain1)
        down_old = act(e[4, 0:8, cut], pl.ds(at + 16, 8), gain1)
        down = act(e[5, 0:8, cut], pl.ds(at + 24, 8), gain1)
        e[0, 0:8, cut] = jnp.concatenate([up_old[0:4], up[0:4]], axis=0)
        e[1, 0:8, cut] = jnp.concatenate([up_old[4:8], up[4:8]], axis=0)
        e[4, 0:8, cut] = jnp.concatenate([down_old[0:4], down[0:4]], axis=0)
        e[5, 0:8, cut] = jnp.concatenate([down_old[4:8], down[4:8]], axis=0)
        for f in range(8):
            if f < 4:
                v = jnp.where(older, prev_ref[f, :, cut], zero)
            else:
                v = x_ref[f - 4, :, cut]
            v = act(v, pl.ds(160 * g + 16 * f, 16), gain1)
            shifted(a1, f, g, v, e[1, f : f + 1, cut], e[4, f : f + 1, cut])
            e[2, f : f + 1, cut] = v[0:1]
            e[3, f : f + 1, cut] = v[15:16]
        for kt in range(3):
            for kh in range(3):
                et[kt, kh, :, pl.ds(PAD + GROUP * g, GROUP)] = jnp.concatenate(
                    [e[kh, kt : kt + 8, cut], e[3 + kh, kt : kt + 8, cut]], axis=0
                ).astype(BF)

    for p, w in enumerate((u0, u1, u2)):
        depth = DEPTHS[p]
        taps = []
        for kt in range(3):
            for kh in range(3):
                parts = []
                for g in range(4):
                    cut = pl.ds(PAD + GROUP * g + STARTS[p], depth)
                    parts.append(a1[kh, kt : kt + 6, :, cut].reshape(96, depth))
                    parts.append(et[kt, kh, :, cut])
                taps.append(jnp.concatenate(parts, axis=0))
        total = jnp.dot(
            jnp.concatenate(taps, axis=1), w[...].reshape(9 * depth, 256), preferred_element_type=F32
        )
        cut = pl.ds(256 * p, 256)
        total = (total + bias1[:, 256 * p : 256 * p + 256]).astype(BF)
        hid[:, cut] = total
        square[0:448, cut] = total * total

    norm(448)
    spot = lax.broadcasted_iota(jnp.int32, (16, GROUP), 0)
    frame = lax.rem(spot, 8)
    keep = ((spot >= 8) | (rows > 0)) & ((spot < 8) | (rows < 15)) & ((frame >= 2) | older)
    for g in range(4):
        cut = pl.ds(GROUP * g, GROUP)
        at = pl.ds(112 * g + 96, 16)
        e[0, :, cut] = jnp.where(keep, act(hid[at, :], at, gain2), 0.0)
        for f in range(6):
            at = pl.ds(112 * g + 16 * f, 16)
            v = act(hid[at, :], at, gain2)
            if f < 2:
                v = jnp.where(older, v, 0.0)
            shifted(a2, f, g, v, e[0, f : f + 1, cut], e[0, 8 + f : 9 + f, cut])

    for p, w in enumerate((v0, v1, v2)):
        depth = DEPTHS[p]
        taps = []
        for kt in range(3):
            for kh in range(3):
                parts = []
                for g in range(4):
                    cut = pl.ds(PAD + GROUP * g + STARTS[p], depth)
                    parts.append(a2[kh, kt : kt + 4, :, cut].reshape(64, depth))
                taps.append(jnp.concatenate(parts, axis=0))
        total = jnp.dot(
            jnp.concatenate(taps, axis=1), w[...].reshape(9 * depth, 256), preferred_element_type=F32
        )
        total = total + bias2[:, 256 * p : 256 * p + 256]
        for g in range(4):
            cut = pl.ds(GROUP * g + 256 * p, 256)
            out_ref[:, :, cut] = (
                x_ref[:, :, cut].astype(F32) + total[64 * g : 64 * g + 64].reshape(4, 16, 256)
            ).astype(BF)


SCRATCH = [
    pltpu.VMEM((640, GROUP), BF),
    pltpu.VMEM((640, GROUP), F32),
    pltpu.VMEM((3, 8, 16, WIDE), BF),
    pltpu.VMEM((6, 16, LANES), F32),
    pltpu.VMEM((3, 3, 16, WIDE), BF),
    pltpu.VMEM((448, GROUP), BF),
    pltpu.VMEM((3, 6, 16, WIDE), BF),
]


def vmem():
    return pl.BlockSpec(memory_space=pltpu.VMEM)


def make_pairs(tms, rws):
    def flat(move):
        pairs = []
        for t in range(tms):
            for r in range(rws):
                to_t, to_r = move(t, r)
                pairs.append((t * rws + r, to_t * rws + to_r))
        return pairs

    def odd(t, r):
        if r in (0, rws - 1):
            return t ^ 1, r
        return t, (r + 1 if r % 2 else r - 1)

    def later(t, r):
        return (t + 1) % tms, r

    def even(t, r):
        return t, r ^ 1

    return (
        flat(later),
        flat(even),
        flat(odd),
        flat(lambda t, r: later(*even(t, r))),
        flat(lambda t, r: ((t + 1) % tms, r) if r in (0, rws - 1) else later(*odd(t, r))),
    )


def block(frames, received, banded):
    near = [pltpu.with_memory_space_constraint(q, pltpu.VMEM) for q in (frames,) + tuple(received) + tuple(banded)]
    return pl.pallas_call(
        main_kernel,
        out_shape=jax.ShapeDtypeStruct((4, 16, LANES), BF),
        in_specs=[vmem()] * 13,
        out_specs=vmem(),
        scratch_shapes=SCRATCH,
        compiler_params=pltpu.CompilerParams(vmem_limit_bytes=24 << 20),
        name="block",
    )(*near)


def solution(mesh):
    later, even_swap, odd_swap, even_later, odd_later = make_pairs(mesh.shape["tm"], mesh.shape["rows"])
    axes = ("tm", "rows")

    def body(frames, gain_one, weight_one, bias_one, gain_two, weight_two, bias_two):
        prev = lax.ppermute(frames, axes, later)
        edge = pltpu.VMEM((8, LANES), BF)
        e0, e1 = pl.pallas_call(
            edges_kernel, out_shape=(edge, edge), in_specs=[vmem()], out_specs=(vmem(), vmem()), name="edges"
        )(frames)
        h0 = lax.ppermute(e0, axes, even_swap)
        h1 = lax.ppermute(e1, axes, odd_swap)
        c0 = lax.ppermute(e0, axes, even_later)
        c1 = lax.ppermute(e1, axes, odd_later)
        banded = bands(weight_one, weight_two, (gain_one, bias_one, gain_two, bias_two))
        return block(frames, (prev, h0, h1, c0, c1), banded)

    in_specs = (P("tm", "rows", None), P(), P(), P(), P(), P(), P())
    out_specs = P("tm", "rows", None)
    return jax.shard_map(body, mesh=mesh, in_specs=in_specs, out_specs=out_specs, check_vma=False)
```

```python
import jax
import jax.numpy as jnp
from jax import lax
from jax.experimental import pallas as pl
from jax.experimental.pallas import tpu as pltpu
from jax.sharding import PartitionSpec as P

C = 96
GROUP = 768
PAD = 128
LANES = 3072
WIDE = LANES + 2 * PAD
STARTS = (-128, 0, 384)
DEPTHS = (512, 768, 512)
HALVES = (
    ((96, (32, 0), (128, 96)), (64, (128, 96), (224, 64))),
    ((32, (96, 64), (192, 32)), (96, (288, 0), (384, 96))),
    ((64, (0, 96), (96, 64)), (32, (96, 64), (192, 32))),
)
BF = jnp.bfloat16
F32 = jnp.float32


def fetch_kernel(x_hbm, e0_ref, e1_ref, x_ref, sems):
    copies = [pltpu.make_async_copy(x_hbm.at[f], x_ref.at[f], sems.at[f]) for f in range(4)]
    for copy in copies:
        copy.start()
    even = lax.rem(lax.axis_index("rows"), 2) == 0
    spot = lax.broadcasted_iota(jnp.int32, (8, LANES), 0)
    top, bot = jnp.zeros((8, LANES), F32), jnp.zeros((8, LANES), F32)
    for f in range(4):
        copies[f].wait()
        head = x_ref[f, 0:8, :].astype(F32)
        tail = x_ref[f, 8:16, :].astype(F32)
        for row in range(2):
            here = spot == 4 * row + f
            top = jnp.where(here, head[row : row + 1], top)
            bot = jnp.where(here, tail[6 + row : 7 + row], bot)
    e0_ref[...] = jnp.where(even, bot, top).astype(BF)
    e1_ref[...] = jnp.where(even, top, bot).astype(BF)


def fetch(frames):
    edge = pltpu.VMEM((8, LANES), BF)
    return pl.pallas_call(
        fetch_kernel,
        out_shape=(edge, edge, pltpu.VMEM((4, 16, LANES), BF)),
        in_specs=[pl.BlockSpec(memory_space=pltpu.HBM)],
        out_specs=(vmem(),) * 3,
        scratch_shapes=[pltpu.SemaphoreType.DMA((4,))],
        compiler_params=pltpu.CompilerParams(vmem_limit_bytes=4 << 20),
        name="fetch",
    )(pltpu.with_memory_space_constraint(frames, pltpu.HBM))


def band_fill(out, p):
    for half in range(2):
        first = HALVES[p][half][1][0]
        cut = slice(128 * half, 128 * half + 128)
        if first:
            out[:, 0:first, cut] = jnp.zeros((9, first, 128), BF)
        end = first + 4 * C
        if end < DEPTHS[p]:
            out[:, end : DEPTHS[p], cut] = jnp.zeros((9, DEPTHS[p] - end, 128), BF)


def band_taps(w_ref, outs, taps):
    lane = lax.broadcasted_iota(jnp.int32, (C, 128), 1)
    none = jnp.zeros((C, 128), BF)
    for k in taps:
        blocks = []
        for kw in range(3):
            wide = jnp.concatenate([w_ref[3 * k + kw].astype(F32), jnp.zeros((C, 32), F32)], axis=1)
            blocks.append({r: (pltpu.roll(wide, r, 1) if r else wide).astype(BF) for r in (0, 32, 64, 96)})
        for p, out in outs:
            for half in range(2):
                edge, left, right = HALVES[p][half]
                for d in range(4):
                    a = blocks[d][left[1]] if d < 3 else none
                    b = blocks[d - 1][right[1]] if d else none
                    row = left[0] + C * d
                    out[k, row : row + C, 128 * half : 128 * half + 128] = jnp.where(lane < edge, a, b)


def band_kernel(
    w1_ref, w2_ref, p0, p1, p2, p3, o0, o1, o2, q0, q1, q2, par_ref, buf, small, sems, small_sems
):
    copies = []
    for n, ref in enumerate((w1_ref, w2_ref)):
        copies.append(pltpu.make_async_copy(ref, buf.at[n], sems.at[n]))
    tiny = [pltpu.make_async_copy(ref, small.at[n], small_sems.at[n]) for n, ref in enumerate((p0, p1, p2, p3))]
    for copy in copies + tiny:
        copy.start()
    both = [list(enumerate(refs)) for refs in ((o0, o1, o2), (q0, q1, q2))]
    for outs in both:
        for p, out in outs:
            band_fill(out, p)
    for n, outs in enumerate(both):
        copies[n].wait()
        band_taps(buf.at[n], outs, range(9))
    for copy in tiny:
        copy.wait()
    params = [0.5 * small[0], small[1], 0.5 * small[2], small[3]]
    par_ref[...] = jnp.concatenate([jnp.concatenate(params, axis=0)] * (GROUP // C), axis=1)


def bands(weight_one, weight_two, params):
    far = [w.reshape(27, C, C) for w in (weight_one, weight_two)] + [q.reshape(1, C) for q in params]
    return pl.pallas_call(
        band_kernel,
        out_shape=tuple(pltpu.VMEM((9, d, 256), BF) for d in DEPTHS * 2) + (pltpu.VMEM((4, GROUP), F32),),
        in_specs=[pl.BlockSpec(memory_space=pltpu.HBM)] * 6,
        out_specs=(vmem(),) * 7,
        scratch_shapes=[
            pltpu.VMEM((2, 27, C, C), BF),
            pltpu.VMEM((4, 1, C), F32),
            pltpu.SemaphoreType.DMA((2,)),
            pltpu.SemaphoreType.DMA((4,)),
        ],
        compiler_params=pltpu.CompilerParams(vmem_limit_bytes=8 << 20),
        cost_estimate=pl.CostEstimate(flops=4000000000, bytes_accessed=18000000, transcendentals=0),
        name="bands",
    )(*[pltpu.with_memory_space_constraint(q, pltpu.HBM) for q in far])


def one_hots():
    lane = lax.broadcasted_iota(jnp.int32, (GROUP, 256), 0)
    col = lax.broadcasted_iota(jnp.int32, (GROUP, 256), 1) * C
    gather = jnp.where((lane >= col) & (lane < col + C), 1.0, 0.0).astype(BF)
    lane = lax.broadcasted_iota(jnp.int32, (256, GROUP), 1)
    col = lax.rem(lax.broadcasted_iota(jnp.int32, (256, GROUP), 0), 128) * C
    spread = jnp.where((lane >= col) & (lane < col + C), 1.0, 0.0).astype(BF)
    return gather, spread


def norm(square, scale, count, gather, spread):
    half = count // 2

    def run(*accs):
        for k in range(3):
            for unit in range(2):
                pltpu.matmul_push_rhs(gather[256 * k : 256 * k + 256, :], k % 2, unit)
                lhs = square[half * unit : half * unit + half, 256 * k : 256 * k + 256]
                pltpu.matmul_acc_lhs(accs[unit], lhs, load_staged_rhs=k % 2)
        for unit in range(2):
            total = pltpu.matmul_pop(accs[unit])[:, 0:128]
            r = lax.rsqrt(total * (1.0 / C) + 1e-06)
            high = r.astype(BF)
            low = (r - high.astype(F32)).astype(BF)
            lhs = jnp.concatenate([high, low], axis=1)
            for n in range(3):
                stage = (n + 1) % 2
                pltpu.matmul_push_rhs(spread[:, 256 * n : 256 * n + 256], stage, unit)
                pltpu.matmul_acc_lhs(accs[unit], lhs, load_staged_rhs=stage)
                scale[half * unit : half * unit + half, 256 * n : 256 * n + 256] = pltpu.matmul_pop(accs[unit])

    pl.run_scoped(run, *[pltpu.ACC(n)((half, 256), F32) for n in range(2)])


def act(v, scale, gain):
    half = v.astype(F32) * scale * gain
    return half + half * jnp.tanh(half)


def zero_sides(ref):
    shape = ref.shape[:-1]
    ref[..., pl.ds(0, PAD)] = jnp.zeros(shape + (PAD,), BF)
    ref[..., pl.ds(PAD + LANES, PAD)] = jnp.zeros(shape + (PAD,), BF)


def shifted(ref, f, g, v, above, below):
    cut = pl.ds(PAD + GROUP * g, GROUP)
    ref[0, f, :, cut] = jnp.concatenate([above, v[0:15]], axis=0).astype(BF)
    ref[1, f, :, cut] = v.astype(BF)
    ref[2, f, :, cut] = jnp.concatenate([v[1:16], below], axis=0).astype(BF)


def groups(ref, index, p, sub):
    lanes = [pl.ds(PAD + GROUP * g + STARTS[p] + 256 * sub, 256) for g in range(4)]
    return jnp.concatenate([ref[index + (slice(None), cut)] for cut in lanes], axis=0)


def convolve(p, weight, users, count):
    def run(*accs):
        step = 0
        for kt in range(3):
            for kh in range(3):
                for sub in range(DEPTHS[p] // 256):
                    unit, stage = step % 2, (step // 2) % 2
                    step += 1
                    pltpu.matmul_push_rhs(weight[3 * kt + kh, 256 * sub : 256 * sub + 256, :], stage, unit)
                    load = stage
                    for chunk, ref, index in users(kt, kh):
                        pltpu.matmul_acc_lhs(
                            accs[2 * chunk + unit], groups(ref, index, p, sub), load_staged_rhs=load
                        )
                        load = None
        return [pltpu.matmul_pop(accs[2 * c]) + pltpu.matmul_pop(accs[2 * c + 1]) for c in range(count)]

    return pl.run_scoped(run, *[pltpu.ACC(n % 2)((64, 256), F32) for n in range(2 * count)])


def inner_kernel(
    x_ref, prev_ref, u0, u1, u2, par_ref, packed_ref, part_ref, ends_ref, gather, spread, a1, square, scale
):
    del packed_ref
    older = lax.axis_index("tm") > 0
    gather[...], spread[...] = one_hots()
    gain1 = par_ref[0:1, :]
    zero_sides(a1)
    zero = jnp.zeros((), BF)
    for g in range(4):
        cut = pl.ds(GROUP * g, GROUP)
        before = jnp.where(older, prev_ref[:, :, cut].reshape(64, GROUP), zero)
        own = x_ref[:, :, cut].reshape(64, GROUP)
        square[128 * g : 128 * g + 64, :] = before * before
        square[128 * g + 64 : 128 * g + 128, :] = own * own
    norm(square, scale, 512, gather, spread)
    none = jnp.zeros((1, GROUP), F32)
    for g in range(4):
        cut = pl.ds(GROUP * g, GROUP)
        for f in range(8):
            if f < 4:
                v = jnp.where(older, prev_ref[f, :, cut], zero)
            else:
                v = x_ref[f - 4, :, cut]
            v = act(v, scale[pl.ds(128 * g + 16 * f, 16), :], gain1)
            shifted(a1, f, g, v, none, none)
            ends_ref[0, f : f + 1, cut] = v[0:1]
            ends_ref[1, f : f + 1, cut] = v[15:16]
    for p, w in enumerate((u0, u1, u2)):
        totals = convolve(p, w, lambda kt, kh: [(f, a1, (kh, f + kt)) for f in range(6)], 6)
        for f, total in enumerate(totals):
            part_ref[64 * f : 64 * f + 64, pl.ds(256 * p, 256)] = total


def main_kernel(
    x_ref, h0_ref, h1_ref, c_ref,
    part_ref, ends_ref, gather, spread, u0, u1, u2, v0, v1, v2, par_ref, out_ref,
    square, scale, e, et, hid, a2,
):
    tm = lax.axis_index("tm")
    rows = lax.axis_index("rows")
    even = lax.rem(rows, 2) == 0
    older = tm > 0
    zero_sides(et)
    zero_sides(a2)
    gain1 = par_ref[0:1, :]
    bias1 = par_ref[1:2, :]
    gain2 = par_ref[2:3, :]
    bias2 = par_ref[3:4, :]

    for g in range(4):
        cut = pl.ds(GROUP * g, GROUP)
        h0, h1 = h0_ref[:, cut].astype(F32), h1_ref[:, cut].astype(F32)
        c0, c1 = c_ref[0:8, cut].astype(F32), c_ref[8:16, cut].astype(F32)
        up = jnp.where(rows > 0, jnp.where(even, h1, h0), 0.0)
        down = jnp.where(rows < 15, jnp.where(even, h0, h1), 0.0)
        up_old = jnp.where((rows > 0) & older, jnp.where(even, c1, c0), 0.0)
        down_old = jnp.where((rows < 15) & older, jnp.where(even, c0, c1), 0.0)
        halo = jnp.concatenate([up_old, up, down_old, down], axis=0).astype(BF)
        e[0, 0:8, cut] = up_old
        e[1, 0:8, cut] = up
        e[4, 0:8, cut] = down_old
        e[5, 0:8, cut] = down
        square[32 * g : 32 * g + 32, :] = halo * halo
    norm(square, scale, 128, gather, spread)
    for g in range(4):
        cut = pl.ds(GROUP * g, GROUP)

        def halo_act(q, n):
            return act(e[q, 0:8, cut], scale[pl.ds(32 * g + 8 * n, 8), :], gain1)

        up_old, up, down_old, down = halo_act(0, 0), halo_act(1, 1), halo_act(4, 2), halo_act(5, 3)
        e[0, 0:8, cut] = jnp.concatenate([up_old[0:4], up[0:4]], axis=0)
        e[1, 0:8, cut] = jnp.concatenate([up_old[4:8], up[4:8]], axis=0)
        e[4, 0:8, cut] = jnp.concatenate([down_old[0:4], down[0:4]], axis=0)
        e[5, 0:8, cut] = jnp.concatenate([down_old[4:8], down[4:8]], axis=0)
        e[2, 0:8, cut] = ends_ref[0, :, cut]
        e[3, 0:8, cut] = ends_ref[1, :, cut]
        for kt in range(3):
            for kh in range(3):
                et[kt, kh, :, pl.ds(PAD + GROUP * g, GROUP)] = jnp.concatenate(
                    [e[kh, kt : kt + 8, cut], e[3 + kh, kt : kt + 8, cut]], axis=0
                ).astype(BF)

    spot = lax.broadcasted_iota(jnp.int32, (16, 256), 0)
    for p, w in enumerate((u0, u1, u2)):

        def users(kt, kh):
            chunks = [(0, et, (kt, kh))]
            if kh != 1:
                chunks.append((1 + kh // 2, et, (kt, 1)))
            return chunks

        lanes = pl.ds(256 * p, 256)
        outside, first, last = convolve(p, w, users, 3)
        bias = bias1[:, 256 * p : 256 * p + 256]
        for f in range(6):
            for g in range(4):
                add = jnp.where(
                    spot == 0,
                    first[16 * g + f : 16 * g + f + 1],
                    jnp.where(spot == 15, last[16 * g + 8 + f : 16 * g + 9 + f], 0.0),
                )
                at = pl.ds(64 * f + 16 * g, 16)
                total = (part_ref[at, lanes] + add + bias).astype(BF)
                hid[at, lanes] = total
                square[at, lanes] = total * total
        total = (outside + bias).astype(BF)
        hid[384:448, lanes] = total
        square[384:448, lanes] = total * total

    norm(square, scale, 448, gather, spread)
    spot = lax.broadcasted_iota(jnp.int32, (16, GROUP), 0)
    frame = lax.rem(spot, 8)
    keep = ((spot >= 8) | (rows > 0)) & ((spot < 8) | (rows < 15)) & ((frame >= 2) | older)
    for g in range(4):
        cut = pl.ds(GROUP * g, GROUP)
        at = pl.ds(384 + 16 * g, 16)
        e[0, :, cut] = jnp.where(keep, act(hid[at, :], scale[at, :], gain2), 0.0)
        for f in range(6):
            at = pl.ds(64 * f + 16 * g, 16)
            v = act(hid[at, :], scale[at, :], gain2)
            if f < 2:
                v = jnp.where(older, v, 0.0)
            shifted(a2, f, g, v, e[0, f : f + 1, cut], e[0, 8 + f : 9 + f, cut])

    for p, w in enumerate((v0, v1, v2)):
        totals = convolve(p, w, lambda kt, kh: [(f, a2, (kh, f + kt)) for f in range(4)], 4)
        for f, total in enumerate(totals):
            total = total + bias2[:, 256 * p : 256 * p + 256]
            for g in range(4):
                cut = pl.ds(GROUP * g + 256 * p, 256)
                out_ref[f, :, cut] = (x_ref[f, :, cut].astype(F32) + total[16 * g : 16 * g + 16]).astype(BF)


SCRATCH = [
    pltpu.VMEM((448, GROUP), BF),
    pltpu.VMEM((448, GROUP), F32),
    pltpu.VMEM((6, 16, LANES), F32),
    pltpu.VMEM((3, 3, 16, WIDE), BF),
    pltpu.VMEM((448, GROUP), BF),
    pltpu.VMEM((3, 6, 16, WIDE), BF),
]


def pack_kernel(h0_ref, h1_ref, par_ref, packed_ref):
    del par_ref
    packed_ref[0:8, :] = h0_ref[...]
    packed_ref[8:16, :] = h1_ref[...]


def pack(*arrays):
    return pl.pallas_call(
        pack_kernel,
        out_shape=pltpu.VMEM((16, LANES), BF),
        in_specs=[vmem()] * 3,
        out_specs=vmem(),
        compiler_params=pltpu.CompilerParams(vmem_limit_bytes=1 << 20),
        name="pack",
    )(*[pltpu.with_memory_space_constraint(q, pltpu.VMEM) for q in arrays])


def inner(*arrays):
    return pl.pallas_call(
        inner_kernel,
        out_shape=(
            pltpu.VMEM((384, GROUP), F32),
            pltpu.VMEM((2, 8, LANES), F32),
            pltpu.VMEM((GROUP, 256), BF),
            pltpu.VMEM((256, GROUP), BF),
        ),
        in_specs=[vmem()] * 7,
        out_specs=(vmem(),) * 4,
        scratch_shapes=[
            pltpu.VMEM((3, 8, 16, WIDE), BF),
            pltpu.VMEM((512, GROUP), BF),
            pltpu.VMEM((512, GROUP), F32),
        ],
        compiler_params=pltpu.CompilerParams(vmem_limit_bytes=12 << 20),
        cost_estimate=pl.CostEstimate(flops=4000000000, bytes_accessed=18000000, transcendentals=0),
        name="inner",
    )(*[pltpu.with_memory_space_constraint(q, pltpu.VMEM) for q in arrays])


def vmem():
    return pl.BlockSpec(memory_space=pltpu.VMEM)


def make_pairs(tms, rws):
    def flat(move):
        pairs = []
        for t in range(tms):
            for r in range(rws):
                to_t, to_r = move(t, r)
                pairs.append((t * rws + r, to_t * rws + to_r))
        return pairs

    def even(t, r):
        return t, r ^ 1

    def odd(t, r):
        if r in (0, rws - 1):
            return t ^ 1, r
        return t, (r + 1 if r % 2 else r - 1)

    def later(t, r):
        return (t + 1, r) if t < tms - 1 else (0, r ^ 1)

    return tuple(flat(move) for move in (later, even, odd))


def block(*arrays):
    near = [pltpu.with_memory_space_constraint(q, pltpu.VMEM) for q in arrays]
    return pl.pallas_call(
        main_kernel,
        out_shape=jax.ShapeDtypeStruct((4, 16, LANES), BF),
        in_specs=[vmem()] * 15,
        out_specs=vmem(),
        scratch_shapes=SCRATCH,
        compiler_params=pltpu.CompilerParams(vmem_limit_bytes=16 << 20),
        name="block",
    )(*near)


def solution(mesh):
    later, even_swap, odd_swap = make_pairs(mesh.shape["tm"], mesh.shape["rows"])
    axes = ("tm", "rows")

    def body(frames, gain_one, weight_one, bias_one, gain_two, weight_two, bias_two):
        prev = lax.ppermute(frames, axes, later)
        e0, e1, near = fetch(frames)
        h0 = lax.ppermute(e0, axes, even_swap)
        h1 = lax.ppermute(e1, axes, odd_swap)
        banded = bands(weight_one, weight_two, (gain_one, bias_one, gain_two, bias_two))
        packed = pack(h0, h1, banded[6])
        corners = lax.ppermute(packed, axes, later)
        partial = inner(near, prev, *banded[:3], banded[6], packed)
        return block(near, h0, h1, corners, *partial, *banded)

    in_specs = (P("tm", "rows", None), P(), P(), P(), P(), P(), P())
    out_specs = P("tm", "rows", None)
    return jax.shard_map(body, mesh=mesh, in_specs=in_specs, out_specs=out_specs, check_vma=False)
```

```python
import jax
import jax.numpy as jnp
from jax import lax
from jax.experimental import pallas as pl
from jax.experimental.pallas import tpu as pltpu
from jax.sharding import PartitionSpec as P

C = 96
GROUP = 768
PAD = 128
LANES = 3072
WIDE = LANES + 2 * PAD
STARTS = (-128, 0, 384)
DEPTHS = (512, 768, 512)
STRIPS = ((96, 0, 96), (64, 96, 64), (32, 64, 32))
STRIP_ROWS = ((32, 128), (96, 288), (0, 96))
BF = jnp.bfloat16
F32 = jnp.float32


def fetch_kernel(x_hbm, e0_ref, e1_ref, x_ref, sems):
    copies = [pltpu.make_async_copy(x_hbm.at[f], x_ref.at[f], sems.at[f]) for f in range(4)]
    for copy in copies:
        copy.start()
    even = lax.rem(lax.axis_index("rows"), 2) == 0
    spot = lax.broadcasted_iota(jnp.int32, (8, LANES), 0)
    top, bot = jnp.zeros((8, LANES), F32), jnp.zeros((8, LANES), F32)
    for f in range(4):
        copies[f].wait()
        head = x_ref[f, 0:8, :].astype(F32)
        tail = x_ref[f, 8:16, :].astype(F32)
        for row in range(2):
            here = spot == 4 * row + f
            top = jnp.where(here, head[row : row + 1], top)
            bot = jnp.where(here, tail[6 + row : 7 + row], bot)
    e0_ref[...] = jnp.where(even, bot, top).astype(BF)
    e1_ref[...] = jnp.where(even, top, bot).astype(BF)


def fetch(frames):
    edge = pltpu.VMEM((8, LANES), BF)
    return pl.pallas_call(
        fetch_kernel,
        out_shape=(edge, edge, pltpu.VMEM((4, 16, LANES), BF)),
        in_specs=[pl.BlockSpec(memory_space=pltpu.HBM)],
        out_specs=(vmem(),) * 3,
        scratch_shapes=[pltpu.SemaphoreType.DMA((4,))],
        compiler_params=pltpu.CompilerParams(vmem_limit_bytes=4 << 20),
        name="fetch",
    )(pltpu.with_memory_space_constraint(frames, pltpu.HBM))


def strips(w_ref, out, taps):
    lane = lax.broadcasted_iota(jnp.int32, (C, 128), 1)
    none = jnp.zeros((C, 128), BF)
    for k in taps:
        blocks = []
        for kw in range(3):
            wide = jnp.concatenate([w_ref[3 * k + kw].astype(F32), jnp.zeros((C, 32), F32)], axis=1)
            blocks.append({r: (pltpu.roll(wide, r, 1) if r else wide).astype(BF) for r in (0, 32, 64, 96)})
        for n, (edge, left, right) in enumerate(STRIPS):
            for d in range(4):
                a = blocks[d][left] if d < 3 else none
                b = blocks[d - 1][right] if d else none
                out[k, n, C * d : C * d + C, :] = jnp.where(lane < edge, a, b)


def weight_tile(ref, k, p, sub):
    halves = []
    for half in range(2):
        low = 256 * sub - STRIP_ROWS[p][half]
        high = low + 256
        parts = []
        if low < 0:
            parts.append(jnp.zeros((min(-low, 256), 128), BF))
        if low < 4 * C and high > 0:
            parts.append(ref[k, (2 * p + half) % 3, max(low, 0) : min(high, 4 * C), :])
        if high > 4 * C:
            parts.append(jnp.zeros((min(high - 4 * C, 256), 128), BF))
        halves.append(jnp.concatenate(parts, axis=0))
    return jnp.concatenate(halves, axis=1)


def band_kernel(w1_ref, w2_ref, p0, p1, p2, p3, u_ref, v_ref, par_ref, buf, small, sems, small_sems):
    copies = []
    for n, ref in enumerate((w1_ref, w2_ref)):
        for kt in range(3):
            part = pl.ds(9 * kt, 9)
            copies.append(pltpu.make_async_copy(ref.at[part], buf.at[n, part], sems.at[n, kt]))
    tiny = [pltpu.make_async_copy(ref, small.at[n], small_sems.at[n]) for n, ref in enumerate((p0, p1, p2, p3))]
    for copy in copies + tiny:
        copy.start()
    for n, out in enumerate((u_ref, v_ref)):
        for kt in range(3):
            copies[3 * n + kt].wait()
            strips(buf.at[n], out, range(3 * kt, 3 * kt + 3))
    for copy in tiny:
        copy.wait()
    params = [0.5 * small[0], small[1], 0.5 * small[2], small[3]]
    par_ref[...] = jnp.concatenate([jnp.concatenate(params, axis=0)] * (GROUP // C), axis=1)


def bands(weight_one, weight_two, params):
    far = [w.reshape(27, C, C) for w in (weight_one, weight_two)] + [q.reshape(1, C) for q in params]
    strip = pltpu.VMEM((9, 3, 4 * C, 128), BF)
    return pl.pallas_call(
        band_kernel,
        out_shape=(strip, strip, pltpu.VMEM((4, GROUP), F32)),
        in_specs=[pl.BlockSpec(memory_space=pltpu.HBM)] * 6,
        out_specs=(vmem(),) * 3,
        scratch_shapes=[
            pltpu.VMEM((2, 27, C, C), BF),
            pltpu.VMEM((4, 1, C), F32),
            pltpu.SemaphoreType.DMA((2, 3)),
            pltpu.SemaphoreType.DMA((4,)),
        ],
        compiler_params=pltpu.CompilerParams(vmem_limit_bytes=8 << 20),
        cost_estimate=pl.CostEstimate(flops=4000000000, bytes_accessed=18000000, transcendentals=0),
        name="bands",
    )(*[pltpu.with_memory_space_constraint(q, pltpu.HBM) for q in far])


def one_hots():
    lane = lax.broadcasted_iota(jnp.int32, (GROUP, 256), 0)
    col = lax.broadcasted_iota(jnp.int32, (GROUP, 256), 1) * C
    gather = jnp.where((lane >= col) & (lane < col + C), 1.0, 0.0).astype(BF)
    lane = lax.broadcasted_iota(jnp.int32, (256, GROUP), 1)
    col = lax.rem(lax.broadcasted_iota(jnp.int32, (256, GROUP), 0), 128) * C
    spread = jnp.where((lane >= col) & (lane < col + C), 1.0, 0.0).astype(BF)
    return gather, spread


def norm(square, scale, count, gather, spread):
    half = count // 2

    def run(*accs):
        for k in range(3):
            for unit in range(2):
                pltpu.matmul_push_rhs(gather[256 * k : 256 * k + 256, :], k % 2, unit)
                lhs = square[half * unit : half * unit + half, 256 * k : 256 * k + 256]
                pltpu.matmul_acc_lhs(accs[unit], lhs, load_staged_rhs=k % 2)
        for unit in range(2):
            total = pltpu.matmul_pop(accs[unit])[:, 0:128]
            r = lax.rsqrt(total * (1.0 / C) + 1e-06)
            high = r.astype(BF)
            low = (r - high.astype(F32)).astype(BF)
            lhs = jnp.concatenate([high, low], axis=1)
            for n in range(3):
                stage = (n + 1) % 2
                pltpu.matmul_push_rhs(spread[:, 256 * n : 256 * n + 256], stage, unit)
                pltpu.matmul_acc_lhs(accs[unit], lhs, load_staged_rhs=stage)
                scale[half * unit : half * unit + half, 256 * n : 256 * n + 256] = pltpu.matmul_pop(accs[unit])

    pl.run_scoped(run, *[pltpu.ACC(n)((half, 256), F32) for n in range(2)])


def act(v, scale, gain):
    half = v.astype(F32) * scale * gain
    return half + half * jnp.tanh(half)


def zero_sides(ref):
    shape = ref.shape[:-1]
    ref[..., pl.ds(0, PAD)] = jnp.zeros(shape + (PAD,), BF)
    ref[..., pl.ds(PAD + LANES, PAD)] = jnp.zeros(shape + (PAD,), BF)


def shifted(ref, f, g, v, above, below):
    cut = pl.ds(PAD + GROUP * g, GROUP)
    ref[0, f, :, cut] = jnp.concatenate([above, v[0:15]], axis=0).astype(BF)
    ref[1, f, :, cut] = v.astype(BF)
    ref[2, f, :, cut] = jnp.concatenate([v[1:16], below], axis=0).astype(BF)


def groups(ref, index, p, sub):
    lanes = [pl.ds(PAD + GROUP * g + STARTS[p] + 256 * sub, 256) for g in range(4)]
    return jnp.concatenate([ref[index + (slice(None), cut)] for cut in lanes], axis=0)


def convolve(p, weight, users, count):
    def run(*accs):
        step = 0
        for kt in range(3):
            for kh in range(3):
                for sub in range(DEPTHS[p] // 256):
                    unit, stage = step % 2, (step // 2) % 2
                    step += 1
                    pltpu.matmul_push_rhs(weight_tile(weight, 3 * kt + kh, p, sub), stage, unit)
                    load = stage
                    for chunk, ref, index in users(kt, kh):
                        pltpu.matmul_acc_lhs(
                            accs[2 * chunk + unit], groups(ref, index, p, sub), load_staged_rhs=load
                        )
                        load = None
        return [pltpu.matmul_pop(accs[2 * c]) + pltpu.matmul_pop(accs[2 * c + 1]) for c in range(count)]

    return pl.run_scoped(run, *[pltpu.ACC(n % 2)((64, 256), F32) for n in range(2 * count)])


def inner_kernel(
    x_ref, prev_ref, u_ref, par_ref, packed_ref, part_ref, ends_ref, gather, spread, a1, square, scale
):
    del packed_ref
    older = lax.axis_index("tm") > 0
    gather[...], spread[...] = one_hots()
    gain1 = par_ref[0:1, :]
    zero_sides(a1)
    zero = jnp.zeros((), BF)
    for g in range(4):
        cut = pl.ds(GROUP * g, GROUP)
        before = jnp.where(older, prev_ref[:, :, cut].reshape(64, GROUP), zero)
        own = x_ref[:, :, cut].reshape(64, GROUP)
        square[128 * g : 128 * g + 64, :] = before * before
        square[128 * g + 64 : 128 * g + 128, :] = own * own
    norm(square, scale, 512, gather, spread)
    none = jnp.zeros((1, GROUP), F32)
    for g in range(4):
        cut = pl.ds(GROUP * g, GROUP)
        for f in range(8):
            if f < 4:
                v = jnp.where(older, prev_ref[f, :, cut], zero)
            else:
                v = x_ref[f - 4, :, cut]
            v = act(v, scale[pl.ds(128 * g + 16 * f, 16), :], gain1)
            shifted(a1, f, g, v, none, none)
            ends_ref[0, f : f + 1, cut] = v[0:1]
            ends_ref[1, f : f + 1, cut] = v[15:16]
    for p in range(3):
        totals = convolve(p, u_ref, lambda kt, kh: [(f, a1, (kh, f + kt)) for f in range(6)], 6)
        for f, total in enumerate(totals):
            part_ref[64 * f : 64 * f + 64, pl.ds(256 * p, 256)] = total


def main_kernel(
    x_ref, h0_ref, h1_ref, c_ref,
    part_ref, ends_ref, gather, spread, u_ref, v_ref, par_ref, out_ref,
    square, scale, e, et, hid, a2,
):
    tm = lax.axis_index("tm")
    rows = lax.axis_index("rows")
    even = lax.rem(rows, 2) == 0
    older = tm > 0
    zero_sides(et)
    zero_sides(a2)
    gain1 = par_ref[0:1, :]
    bias1 = par_ref[1:2, :]
    gain2 = par_ref[2:3, :]
    bias2 = par_ref[3:4, :]

    for g in range(4):
        cut = pl.ds(GROUP * g, GROUP)
        h0, h1 = h0_ref[:, cut].astype(F32), h1_ref[:, cut].astype(F32)
        c0, c1 = c_ref[0:8, cut].astype(F32), c_ref[8:16, cut].astype(F32)
        up = jnp.where(rows > 0, jnp.where(even, h1, h0), 0.0)
        down = jnp.where(rows < 15, jnp.where(even, h0, h1), 0.0)
        up_old = jnp.where((rows > 0) & older, jnp.where(even, c1, c0), 0.0)
        down_old = jnp.where((rows < 15) & older, jnp.where(even, c0, c1), 0.0)
        halo = jnp.concatenate([up_old, up, down_old, down], axis=0).astype(BF)
        e[0, 0:8, cut] = up_old
        e[1, 0:8, cut] = up
        e[4, 0:8, cut] = down_old
        e[5, 0:8, cut] = down
        square[32 * g : 32 * g + 32, :] = halo * halo
    norm(square, scale, 128, gather, spread)
    for g in range(4):
        cut = pl.ds(GROUP * g, GROUP)

        def halo_act(q, n):
            return act(e[q, 0:8, cut], scale[pl.ds(32 * g + 8 * n, 8), :], gain1)

        up_old, up, down_old, down = halo_act(0, 0), halo_act(1, 1), halo_act(4, 2), halo_act(5, 3)
        e[0, 0:8, cut] = jnp.concatenate([up_old[0:4], up[0:4]], axis=0)
        e[1, 0:8, cut] = jnp.concatenate([up_old[4:8], up[4:8]], axis=0)
        e[4, 0:8, cut] = jnp.concatenate([down_old[0:4], down[0:4]], axis=0)
        e[5, 0:8, cut] = jnp.concatenate([down_old[4:8], down[4:8]], axis=0)
        e[2, 0:8, cut] = ends_ref[0, :, cut]
        e[3, 0:8, cut] = ends_ref[1, :, cut]
        for kt in range(3):
            for kh in range(3):
                et[kt, kh, :, pl.ds(PAD + GROUP * g, GROUP)] = jnp.concatenate(
                    [e[kh, kt : kt + 8, cut], e[3 + kh, kt : kt + 8, cut]], axis=0
                ).astype(BF)

    spot = lax.broadcasted_iota(jnp.int32, (16, 256), 0)
    for p in range(3):

        def users(kt, kh):
            chunks = [(0, et, (kt, kh))]
            if kh != 1:
                chunks.append((1 + kh // 2, et, (kt, 1)))
            return chunks

        lanes = pl.ds(256 * p, 256)
        outside, first, last = convolve(p, u_ref, users, 3)
        bias = bias1[:, 256 * p : 256 * p + 256]
        for f in range(6):
            for g in range(4):
                add = jnp.where(
                    spot == 0,
                    first[16 * g + f : 16 * g + f + 1],
                    jnp.where(spot == 15, last[16 * g + 8 + f : 16 * g + 9 + f], 0.0),
                )
                at = pl.ds(64 * f + 16 * g, 16)
                total = (part_ref[at, lanes] + add + bias).astype(BF)
                hid[at, lanes] = total
                square[at, lanes] = total * total
        total = (outside + bias).astype(BF)
        hid[384:448, lanes] = total
        square[384:448, lanes] = total * total

    norm(square, scale, 448, gather, spread)
    spot = lax.broadcasted_iota(jnp.int32, (16, GROUP), 0)
    frame = lax.rem(spot, 8)
    keep = ((spot >= 8) | (rows > 0)) & ((spot < 8) | (rows < 15)) & ((frame >= 2) | older)
    for g in range(4):
        cut = pl.ds(GROUP * g, GROUP)
        at = pl.ds(384 + 16 * g, 16)
        e[0, :, cut] = jnp.where(keep, act(hid[at, :], scale[at, :], gain2), 0.0)
        for f in range(6):
            at = pl.ds(64 * f + 16 * g, 16)
            v = act(hid[at, :], scale[at, :], gain2)
            if f < 2:
                v = jnp.where(older, v, 0.0)
            shifted(a2, f, g, v, e[0, f : f + 1, cut], e[0, 8 + f : 9 + f, cut])

    for p in range(3):
        totals = convolve(p, v_ref, lambda kt, kh: [(f, a2, (kh, f + kt)) for f in range(4)], 4)
        for f, total in enumerate(totals):
            total = total + bias2[:, 256 * p : 256 * p + 256]
            for g in range(4):
                cut = pl.ds(GROUP * g + 256 * p, 256)
                out_ref[f, :, cut] = (x_ref[f, :, cut].astype(F32) + total[16 * g : 16 * g + 16]).astype(BF)


SCRATCH = [
    pltpu.VMEM((448, GROUP), BF),
    pltpu.VMEM((448, GROUP), F32),
    pltpu.VMEM((6, 16, LANES), F32),
    pltpu.VMEM((3, 3, 16, WIDE), BF),
    pltpu.VMEM((448, GROUP), BF),
    pltpu.VMEM((3, 6, 16, WIDE), BF),
]


def pack_kernel(h0_ref, h1_ref, par_ref, packed_ref):
    del par_ref
    packed_ref[0:8, :] = h0_ref[...]
    packed_ref[8:16, :] = h1_ref[...]


def pack(*arrays):
    return pl.pallas_call(
        pack_kernel,
        out_shape=pltpu.VMEM((16, LANES), BF),
        in_specs=[vmem()] * 3,
        out_specs=vmem(),
        compiler_params=pltpu.CompilerParams(vmem_limit_bytes=1 << 20),
        name="pack",
    )(*[pltpu.with_memory_space_constraint(q, pltpu.VMEM) for q in arrays])


def inner(*arrays):
    return pl.pallas_call(
        inner_kernel,
        out_shape=(
            pltpu.VMEM((384, GROUP), F32),
            pltpu.VMEM((2, 8, LANES), F32),
            pltpu.VMEM((GROUP, 256), BF),
            pltpu.VMEM((256, GROUP), BF),
        ),
        in_specs=[vmem()] * 5,
        out_specs=(vmem(),) * 4,
        scratch_shapes=[
            pltpu.VMEM((3, 8, 16, WIDE), BF),
            pltpu.VMEM((512, GROUP), BF),
            pltpu.VMEM((512, GROUP), F32),
        ],
        compiler_params=pltpu.CompilerParams(vmem_limit_bytes=12 << 20),
        cost_estimate=pl.CostEstimate(flops=4000000000, bytes_accessed=18000000, transcendentals=0),
        name="inner",
    )(*[pltpu.with_memory_space_constraint(q, pltpu.VMEM) for q in arrays])


def vmem():
    return pl.BlockSpec(memory_space=pltpu.VMEM)


def make_pairs(tms, rws):
    def flat(move):
        pairs = []
        for t in range(tms):
            for r in range(rws):
                to_t, to_r = move(t, r)
                pairs.append((t * rws + r, to_t * rws + to_r))
        return pairs

    def even(t, r):
        return t, r ^ 1

    def odd(t, r):
        if r in (0, rws - 1):
            return t ^ 1, r
        return t, (r + 1 if r % 2 else r - 1)

    def later(t, r):
        return (t + 1, r) if t < tms - 1 else (0, r ^ 1)

    return tuple(flat(move) for move in (later, even, odd))


def block(*arrays):
    near = [pltpu.with_memory_space_constraint(q, pltpu.VMEM) for q in arrays]
    return pl.pallas_call(
        main_kernel,
        out_shape=jax.ShapeDtypeStruct((4, 16, LANES), BF),
        in_specs=[vmem()] * 11,
        out_specs=vmem(),
        scratch_shapes=SCRATCH,
        compiler_params=pltpu.CompilerParams(vmem_limit_bytes=16 << 20),
        name="block",
    )(*near)


def solution(mesh):
    later, even_swap, odd_swap = make_pairs(mesh.shape["tm"], mesh.shape["rows"])
    axes = ("tm", "rows")

    def body(frames, gain_one, weight_one, bias_one, gain_two, weight_two, bias_two):
        prev = lax.ppermute(frames, axes, later)
        e0, e1, near = fetch(frames)
        h0 = lax.ppermute(e0, axes, even_swap)
        h1 = lax.ppermute(e1, axes, odd_swap)
        banded = bands(weight_one, weight_two, (gain_one, bias_one, gain_two, bias_two))
        packed = pack(h0, h1, banded[2])
        corners = lax.ppermute(packed, axes, later)
        partial = inner(near, prev, banded[0], banded[2], packed)
        return block(near, h0, h1, corners, *partial, *banded)

    in_specs = (P("tm", "rows", None), P(), P(), P(), P(), P(), P())
    out_specs = P("tm", "rows", None)
    return jax.shard_map(body, mesh=mesh, in_specs=in_specs, out_specs=out_specs, check_vma=False)
```

```python
import jax
import jax.numpy as jnp
from jax import lax
from jax.experimental import pallas as pl
from jax.experimental.pallas import tpu as pltpu
from jax.sharding import PartitionSpec as P

C = 96
GROUP = 768
PAD = 128
LANES = 3072
WIDE = LANES + 2 * PAD
STARTS = (-128, 0, 384)
DEPTHS = (512, 768, 512)
STRIPS = ((96, 0, 96), (64, 96, 64), (32, 64, 32))
STRIP_ROWS = ((32, 128), (96, 288), (0, 96))
BF = jnp.bfloat16
F32 = jnp.float32


def fetch_kernel(x_hbm, e0_ref, e1_ref, x_ref, sems):
    copies = [pltpu.make_async_copy(x_hbm.at[f], x_ref.at[f], sems.at[f]) for f in range(4)]
    for copy in copies:
        copy.start()
    even = lax.rem(lax.axis_index("rows"), 2) == 0
    spot = lax.broadcasted_iota(jnp.int32, (8, LANES), 0)
    top, bot = jnp.zeros((8, LANES), F32), jnp.zeros((8, LANES), F32)
    for f in range(4):
        copies[f].wait()
        head = x_ref[f, 0:8, :].astype(F32)
        tail = x_ref[f, 8:16, :].astype(F32)
        for row in range(2):
            here = spot == 4 * row + f
            top = jnp.where(here, head[row : row + 1], top)
            bot = jnp.where(here, tail[6 + row : 7 + row], bot)
    e0_ref[...] = jnp.where(even, bot, top).astype(BF)
    e1_ref[...] = jnp.where(even, top, bot).astype(BF)


def fetch(frames):
    edge = pltpu.VMEM((8, LANES), BF)
    return pl.pallas_call(
        fetch_kernel,
        out_shape=(edge, edge, pltpu.VMEM((4, 16, LANES), BF)),
        in_specs=[pl.BlockSpec(memory_space=pltpu.HBM)],
        out_specs=(vmem(),) * 3,
        scratch_shapes=[pltpu.SemaphoreType.DMA((4,))],
        compiler_params=pltpu.CompilerParams(vmem_limit_bytes=4 << 20),
        name="fetch",
    )(pltpu.with_memory_space_constraint(frames, pltpu.HBM))


def strips(w_ref, out, taps):
    lane = lax.broadcasted_iota(jnp.int32, (C, 128), 1)
    none = jnp.zeros((C, 128), BF)
    for k in taps:
        blocks = []
        for kw in range(3):
            wide = jnp.concatenate([w_ref[3 * k + kw].astype(F32), jnp.zeros((C, 32), F32)], axis=1)
            blocks.append({r: (pltpu.roll(wide, r, 1) if r else wide).astype(BF) for r in (0, 32, 64, 96)})
        for n, (edge, left, right) in enumerate(STRIPS):
            for d in range(4):
                a = blocks[d][left] if d < 3 else none
                b = blocks[d - 1][right] if d else none
                out[k, n, C * d : C * d + C, :] = jnp.where(lane < edge, a, b)


def weight_tile(ref, k, p, sub):
    halves = []
    for half in range(2):
        low = 256 * sub - STRIP_ROWS[p][half]
        high = low + 256
        parts = []
        if low < 0:
            parts.append(jnp.zeros((min(-low, 256), 128), BF))
        if low < 4 * C and high > 0:
            parts.append(ref[k, (2 * p + half) % 3, max(low, 0) : min(high, 4 * C), :])
        if high > 4 * C:
            parts.append(jnp.zeros((min(high - 4 * C, 256), 128), BF))
        halves.append(jnp.concatenate(parts, axis=0))
    return jnp.concatenate(halves, axis=1)


def band_kernel(w1_ref, w2_ref, p0, p1, p2, p3, u_ref, v_ref, par_ref, buf, small, sems, small_sems):
    copies = []
    for n, ref in enumerate((w1_ref, w2_ref)):
        for kt in range(3):
            part = pl.ds(9 * kt, 9)
            copies.append(pltpu.make_async_copy(ref.at[part], buf.at[n, part], sems.at[n, kt]))
    tiny = [pltpu.make_async_copy(ref, small.at[n], small_sems.at[n]) for n, ref in enumerate((p0, p1, p2, p3))]
    for copy in copies + tiny:
        copy.start()
    for n, out in enumerate((u_ref, v_ref)):
        for kt in range(3):
            copies[3 * n + kt].wait()
            strips(buf.at[n], out, range(3 * kt, 3 * kt + 3))
    for copy in tiny:
        copy.wait()
    params = [0.5 * small[0], small[1], 0.5 * small[2], small[3]]
    par_ref[...] = jnp.concatenate([jnp.concatenate(params, axis=0)] * (GROUP // C), axis=1)


def bands(weight_one, weight_two, params):
    far = [w.reshape(27, C, C) for w in (weight_one, weight_two)] + [q.reshape(1, C) for q in params]
    strip = pltpu.VMEM((9, 3, 4 * C, 128), BF)
    return pl.pallas_call(
        band_kernel,
        out_shape=(strip, strip, pltpu.VMEM((4, GROUP), F32)),
        in_specs=[pl.BlockSpec(memory_space=pltpu.HBM)] * 6,
        out_specs=(vmem(),) * 3,
        scratch_shapes=[
            pltpu.VMEM((2, 27, C, C), BF),
            pltpu.VMEM((4, 1, C), F32),
            pltpu.SemaphoreType.DMA((2, 3)),
            pltpu.SemaphoreType.DMA((4,)),
        ],
        compiler_params=pltpu.CompilerParams(vmem_limit_bytes=8 << 20),
        cost_estimate=pl.CostEstimate(flops=4000000000, bytes_accessed=18000000, transcendentals=0),
        name="bands",
    )(*[pltpu.with_memory_space_constraint(q, pltpu.HBM) for q in far])


def one_hots():
    lane = lax.broadcasted_iota(jnp.int32, (GROUP, 256), 0)
    col = lax.broadcasted_iota(jnp.int32, (GROUP, 256), 1) * C
    gather = jnp.where((lane >= col) & (lane < col + C), 1.0, 0.0).astype(BF)
    lane = lax.broadcasted_iota(jnp.int32, (256, GROUP), 1)
    col = lax.rem(lax.broadcasted_iota(jnp.int32, (256, GROUP), 0), 128) * C
    spread = jnp.where((lane >= col) & (lane < col + C), 1.0, 0.0).astype(BF)
    return gather, spread


def norm(square, scale, count, gather, spread):
    half = count // 2

    def run(*accs):
        for k in range(3):
            for unit in range(2):
                pltpu.matmul_push_rhs(gather[256 * k : 256 * k + 256, :], k % 2, unit)
                lhs = square[half * unit : half * unit + half, 256 * k : 256 * k + 256]
                pltpu.matmul_acc_lhs(accs[3 * unit], lhs, load_staged_rhs=k % 2)
        left = []
        for unit in range(2):
            total = pltpu.matmul_pop(accs[3 * unit])[:, 0:128]
            r = lax.rsqrt(total * (1.0 / C) + 1e-06)
            high = r.astype(BF)
            low = (r - high.astype(F32)).astype(BF)
            left.append(jnp.concatenate([high, low], axis=1))
        for n in range(3):
            for unit in range(2):
                stage = (n + 1) % 2
                pltpu.matmul_push_rhs(spread[:, 256 * n : 256 * n + 256], stage, unit)
                pltpu.matmul_acc_lhs(accs[3 * unit + n], left[unit], load_staged_rhs=stage)
        for n in range(3):
            for unit in range(2):
                rows = pl.ds(half * unit, half)
                scale[rows, 256 * n : 256 * n + 256] = pltpu.matmul_pop(accs[3 * unit + n])

    pl.run_scoped(run, *[pltpu.ACC(n // 3)((half, 256), F32) for n in range(6)])


def act(v, scale, gain):
    half = v.astype(F32) * scale * gain
    return half + half * jnp.tanh(half)


def zero_sides(ref):
    shape = ref.shape[:-1]
    ref[..., pl.ds(0, PAD)] = jnp.zeros(shape + (PAD,), BF)
    ref[..., pl.ds(PAD + LANES, PAD)] = jnp.zeros(shape + (PAD,), BF)


def shifted(ref, f, g, v, above, below):
    cut = pl.ds(PAD + GROUP * g, GROUP)
    ref[0, f, :, cut] = jnp.concatenate([above, v[0:15]], axis=0).astype(BF)
    ref[1, f, :, cut] = v.astype(BF)
    ref[2, f, :, cut] = jnp.concatenate([v[1:16], below], axis=0).astype(BF)


def groups(ref, index, p, sub):
    lanes = [pl.ds(PAD + GROUP * g + STARTS[p] + 256 * sub, 256) for g in range(4)]
    return jnp.concatenate([ref[index + (slice(None), cut)] for cut in lanes], axis=0)


def convolve(p, weight, users, count):
    def run(*accs):
        step = 0
        for kt in range(3):
            for kh in range(3):
                for sub in range(DEPTHS[p] // 256):
                    unit, stage = step % 2, (step // 2) % 2
                    step += 1
                    pltpu.matmul_push_rhs(weight_tile(weight, 3 * kt + kh, p, sub), stage, unit)
                    load = stage
                    for chunk, ref, index in users(kt, kh):
                        pltpu.matmul_acc_lhs(
                            accs[2 * chunk + unit], groups(ref, index, p, sub), load_staged_rhs=load
                        )
                        load = None
        return [pltpu.matmul_pop(accs[2 * c]) + pltpu.matmul_pop(accs[2 * c + 1]) for c in range(count)]

    return pl.run_scoped(run, *[pltpu.ACC(n % 2)((64, 256), F32) for n in range(2 * count)])


def inner_kernel(
    x_ref, prev_ref, u_ref, par_ref, packed_ref, part_ref, ends_ref, gather, spread, a1, square, scale
):
    del packed_ref
    older = lax.axis_index("tm") > 0
    gather[...], spread[...] = one_hots()
    gain1 = par_ref[0:1, :]
    zero_sides(a1)
    zero = jnp.zeros((), BF)
    for g in range(4):
        cut = pl.ds(GROUP * g, GROUP)
        before = jnp.where(older, prev_ref[:, :, cut].reshape(64, GROUP), zero)
        own = x_ref[:, :, cut].reshape(64, GROUP)
        square[128 * g : 128 * g + 64, :] = before * before
        square[128 * g + 64 : 128 * g + 128, :] = own * own
    norm(square, scale, 512, gather, spread)
    none = jnp.zeros((1, GROUP), F32)
    for g in range(4):
        cut = pl.ds(GROUP * g, GROUP)
        for f in range(8):
            if f < 4:
                v = jnp.where(older, prev_ref[f, :, cut], zero)
            else:
                v = x_ref[f - 4, :, cut]
            v = act(v, scale[pl.ds(128 * g + 16 * f, 16), :], gain1)
            shifted(a1, f, g, v, none, none)
            ends_ref[0, f : f + 1, cut] = v[0:1]
            ends_ref[1, f : f + 1, cut] = v[15:16]
    for p in range(3):
        totals = convolve(p, u_ref, lambda kt, kh: [(f, a1, (kh, f + kt)) for f in range(6)], 6)
        for f, total in enumerate(totals):
            part_ref[64 * f : 64 * f + 64, pl.ds(256 * p, 256)] = total


def main_kernel(
    x_ref, h0_ref, h1_ref, c_ref,
    part_ref, ends_ref, gather, spread, u_ref, v_ref, par_ref, out_ref,
    square, scale, e, et, hid, a2,
):
    tm = lax.axis_index("tm")
    rows = lax.axis_index("rows")
    even = lax.rem(rows, 2) == 0
    older = tm > 0
    zero_sides(et)
    zero_sides(a2)
    gain1 = par_ref[0:1, :]
    bias1 = par_ref[1:2, :]
    gain2 = par_ref[2:3, :]
    bias2 = par_ref[3:4, :]

    for g in range(4):
        cut = pl.ds(GROUP * g, GROUP)
        h0, h1 = h0_ref[:, cut].astype(F32), h1_ref[:, cut].astype(F32)
        c0, c1 = c_ref[0:8, cut].astype(F32), c_ref[8:16, cut].astype(F32)
        up = jnp.where(rows > 0, jnp.where(even, h1, h0), 0.0)
        down = jnp.where(rows < 15, jnp.where(even, h0, h1), 0.0)
        up_old = jnp.where((rows > 0) & older, jnp.where(even, c1, c0), 0.0)
        down_old = jnp.where((rows < 15) & older, jnp.where(even, c0, c1), 0.0)
        halo = jnp.concatenate([up_old, up, down_old, down], axis=0).astype(BF)
        e[0, 0:8, cut] = up_old
        e[1, 0:8, cut] = up
        e[4, 0:8, cut] = down_old
        e[5, 0:8, cut] = down
        square[32 * g : 32 * g + 32, :] = halo * halo
    norm(square, scale, 128, gather, spread)
    for g in range(4):
        cut = pl.ds(GROUP * g, GROUP)

        def halo_act(q, n):
            return act(e[q, 0:8, cut], scale[pl.ds(32 * g + 8 * n, 8), :], gain1)

        up_old, up, down_old, down = halo_act(0, 0), halo_act(1, 1), halo_act(4, 2), halo_act(5, 3)
        e[0, 0:8, cut] = jnp.concatenate([up_old[0:4], up[0:4]], axis=0)
        e[1, 0:8, cut] = jnp.concatenate([up_old[4:8], up[4:8]], axis=0)
        e[4, 0:8, cut] = jnp.concatenate([down_old[0:4], down[0:4]], axis=0)
        e[5, 0:8, cut] = jnp.concatenate([down_old[4:8], down[4:8]], axis=0)
        e[2, 0:8, cut] = ends_ref[0, :, cut]
        e[3, 0:8, cut] = ends_ref[1, :, cut]
        for kt in range(3):
            for kh in range(3):
                et[kt, kh, :, pl.ds(PAD + GROUP * g, GROUP)] = jnp.concatenate(
                    [e[kh, kt : kt + 8, cut], e[3 + kh, kt : kt + 8, cut]], axis=0
                ).astype(BF)

    spot = lax.broadcasted_iota(jnp.int32, (16, 256), 0)
    for p in range(3):

        def users(kt, kh):
            chunks = [(0, et, (kt, kh))]
            if kh != 1:
                chunks.append((1 + kh // 2, et, (kt, 1)))
            return chunks

        lanes = pl.ds(256 * p, 256)
        outside, first, last = convolve(p, u_ref, users, 3)
        bias = bias1[:, 256 * p : 256 * p + 256]
        for f in range(6):
            for g in range(4):
                add = jnp.where(
                    spot == 0,
                    first[16 * g + f : 16 * g + f + 1],
                    jnp.where(spot == 15, last[16 * g + 8 + f : 16 * g + 9 + f], 0.0),
                )
                at = pl.ds(64 * f + 16 * g, 16)
                total = (part_ref[at, lanes] + add + bias).astype(BF)
                hid[at, lanes] = total
                square[at, lanes] = total * total
        total = (outside + bias).astype(BF)
        hid[384:448, lanes] = total
        square[384:448, lanes] = total * total

    norm(square, scale, 448, gather, spread)
    spot = lax.broadcasted_iota(jnp.int32, (16, GROUP), 0)
    frame = lax.rem(spot, 8)
    keep = ((spot >= 8) | (rows > 0)) & ((spot < 8) | (rows < 15)) & ((frame >= 2) | older)
    for g in range(4):
        cut = pl.ds(GROUP * g, GROUP)
        at = pl.ds(384 + 16 * g, 16)
        e[0, :, cut] = jnp.where(keep, act(hid[at, :], scale[at, :], gain2), 0.0)
        for f in range(6):
            at = pl.ds(64 * f + 16 * g, 16)
            v = act(hid[at, :], scale[at, :], gain2)
            if f < 2:
                v = jnp.where(older, v, 0.0)
            shifted(a2, f, g, v, e[0, f : f + 1, cut], e[0, 8 + f : 9 + f, cut])

    for p in range(3):
        totals = convolve(p, v_ref, lambda kt, kh: [(f, a2, (kh, f + kt)) for f in range(4)], 4)
        for f, total in enumerate(totals):
            total = total + bias2[:, 256 * p : 256 * p + 256]
            for g in range(4):
                cut = pl.ds(GROUP * g + 256 * p, 256)
                out_ref[f, :, cut] = (x_ref[f, :, cut].astype(F32) + total[16 * g : 16 * g + 16]).astype(BF)


SCRATCH = [
    pltpu.VMEM((448, GROUP), BF),
    pltpu.VMEM((448, GROUP), F32),
    pltpu.VMEM((6, 16, LANES), F32),
    pltpu.VMEM((3, 3, 16, WIDE), BF),
    pltpu.VMEM((448, GROUP), BF),
    pltpu.VMEM((3, 6, 16, WIDE), BF),
]


def pack_kernel(h0_ref, h1_ref, par_ref, packed_ref):
    del par_ref
    packed_ref[0:8, :] = h0_ref[...]
    packed_ref[8:16, :] = h1_ref[...]


def pack(*arrays):
    return pl.pallas_call(
        pack_kernel,
        out_shape=pltpu.VMEM((16, LANES), BF),
        in_specs=[vmem()] * 3,
        out_specs=vmem(),
        compiler_params=pltpu.CompilerParams(vmem_limit_bytes=1 << 20),
        name="pack",
    )(*[pltpu.with_memory_space_constraint(q, pltpu.VMEM) for q in arrays])


def inner(*arrays):
    return pl.pallas_call(
        inner_kernel,
        out_shape=(
            pltpu.VMEM((384, GROUP), F32),
            pltpu.VMEM((2, 8, LANES), F32),
            pltpu.VMEM((GROUP, 256), BF),
            pltpu.VMEM((256, GROUP), BF),
        ),
        in_specs=[vmem()] * 5,
        out_specs=(vmem(),) * 4,
        scratch_shapes=[
            pltpu.VMEM((3, 8, 16, WIDE), BF),
            pltpu.VMEM((512, GROUP), BF),
            pltpu.VMEM((512, GROUP), F32),
        ],
        compiler_params=pltpu.CompilerParams(vmem_limit_bytes=12 << 20),
        cost_estimate=pl.CostEstimate(flops=4000000000, bytes_accessed=18000000, transcendentals=0),
        name="inner",
    )(*[pltpu.with_memory_space_constraint(q, pltpu.VMEM) for q in arrays])


def vmem():
    return pl.BlockSpec(memory_space=pltpu.VMEM)


def make_pairs(tms, rws):
    def flat(move):
        pairs = []
        for t in range(tms):
            for r in range(rws):
                to_t, to_r = move(t, r)
                pairs.append((t * rws + r, to_t * rws + to_r))
        return pairs

    def even(t, r):
        return t, r ^ 1

    def odd(t, r):
        if r in (0, rws - 1):
            return t ^ 1, r
        return t, (r + 1 if r % 2 else r - 1)

    def later(t, r):
        return (t + 1, r) if t < tms - 1 else (0, r ^ 1)

    return tuple(flat(move) for move in (later, even, odd))


def block(*arrays):
    near = [pltpu.with_memory_space_constraint(q, pltpu.VMEM) for q in arrays]
    return pl.pallas_call(
        main_kernel,
        out_shape=jax.ShapeDtypeStruct((4, 16, LANES), BF),
        in_specs=[vmem()] * 11,
        out_specs=vmem(),
        scratch_shapes=SCRATCH,
        compiler_params=pltpu.CompilerParams(vmem_limit_bytes=16 << 20),
        name="block",
    )(*near)


def solution(mesh):
    later, even_swap, odd_swap = make_pairs(mesh.shape["tm"], mesh.shape["rows"])
    axes = ("tm", "rows")

    def body(frames, gain_one, weight_one, bias_one, gain_two, weight_two, bias_two):
        e0, e1, near = fetch(frames)
        prev = lax.ppermute(near, axes, later)
        h0 = lax.ppermute(e0, axes, even_swap)
        h1 = lax.ppermute(e1, axes, odd_swap)
        banded = bands(weight_one, weight_two, (gain_one, bias_one, gain_two, bias_two))
        packed = pack(h0, h1, banded[2])
        corners = lax.ppermute(packed, axes, later)
        partial = inner(near, prev, banded[0], banded[2], packed)
        return block(near, h0, h1, corners, *partial, *banded)

    in_specs = (P("tm", "rows", None), P(), P(), P(), P(), P(), P())
    out_specs = P("tm", "rows", None)
    return jax.shard_map(body, mesh=mesh, in_specs=in_specs, out_specs=out_specs, check_vma=False)
```
